256 devices in a mesh: freq: 16 (over y_lo, z), obs: 16 (over x, y_hi, core).
Axes of the slice: x: 4, y: 4 (y_hi: 2, y_lo: 2; y = y_hi * 2 + y_lo), z: 8, core: 2. Of those that a mesh axis runs over, the one named last changes fastest.
Arguments:
- samples: bfloat16 [4, 2048, 8192], P(None, 'freq', 'obs'), may hold values from -6 to 6
- panel_geom: float32 [4, 8192], P(None, 'obs'), may hold values from -1 to 2, as said below
- panel_slot: int32 [16, 512], P('obs'), may hold values from 0 to 511, each once within a row
- observer_pos: float32 [3, 4096], P(None, 'obs'), may hold values from -4 to 4, as said below
- observer_slot: int32 [16, 256], P('obs'), may hold values from 0 to 255, each once within a row
Outputs:
- pressure: float32 [4096, 64, 2, 16], P('obs', 'freq')
The draws below stay inside these ranges and needn't reach their ends.
Inputs may be any that keep to these rules, and one draw needn't show every extreme that they name: `panel_geom`: panel centres lie in the cube of half side 1 about the anchor; areas lie in 0.5 to 2. `observer_pos`: observers lie between radius 2.5 and 4 from the anchor. `panel_slot`: each row is a reordering of 0 to 511. `observer_slot`: each row is a reordering of 0 to 255.
All inputs are finite; a program needn't handle non-finite values.
Results may differ from the reference program's by a relative error of at most 0.0051.
Values may be sent and summed in bfloat16 or wider, within the bound.
A program may use at most 64 MiB of HBM per device.

```python
import math
import jax
import jax.numpy as jnp
from jax import lax

WIN = 128
FREQS = 64
SEGS = 16
TIMES = 2048
PAN_OBS = 512
PANELS = 8192
OBS_DEV = 256
OBSERVERS = 4096
N_OBS = 16


def draw_panel_geom(key, part):
    key = jax.random.fold_in(key, 11)
    place_key, area_key = jax.random.split(key)
    position = jax.random.uniform(place_key, (3, PANELS), jnp.float32, -1.0, 1.0)
    panel_area = jnp.exp(jax.random.uniform(area_key, (1, PANELS), jnp.float32, math.log(0.5), math.log(2.0)))
    return jnp.concatenate([position, panel_area], 0)


def draw_observer_pos(key, part):
    key = jax.random.fold_in(key, 23)
    radius_key, polar_key, turn_key = jax.random.split(key, 3)
    radius = jax.random.uniform(radius_key, (OBSERVERS,), jnp.float32, 2.5, 4.0)
    cosine = jax.random.uniform(polar_key, (OBSERVERS,), jnp.float32, -1.0, 1.0)
    azimuth = jax.random.uniform(turn_key, (OBSERVERS,), jnp.float32, -math.pi, math.pi)
    sine = jnp.sqrt(jnp.maximum(1.0 - cosine * cosine, 0.0))
    return jnp.stack([radius * sine * jnp.cos(azimuth), radius * sine * jnp.sin(azimuth), radius * cosine], 0)


def shard_levels(rng, shape, cuts, low, top_value):
    def one(axis_at, blocks):
        steps = jax.random.uniform(jax.random.fold_in(jax.random.fold_in(rng, 6), axis_at), (blocks,), jnp.float32, low / len(cuts), top_value / len(cuts))
        return jnp.repeat(jnp.exp(steps), shape[axis_at] // blocks).reshape((-1,) + (1,) * (len(shape) - axis_at - 1))

    loudness = one(*cuts[0])
    for cut in cuts[1:]:
        loudness = loudness * one(*cut)
    return loudness


def centred(stream_key, extent, spread, most, shards=(), held_as=jnp.bfloat16):
    factor_of = shard_levels(stream_key, extent, shards, -0.22, 0.18) if shards else 1.0
    array = jax.random.normal(stream_key, extent, jnp.float32) * spread * factor_of
    return jnp.minimum(jnp.maximum(array, -most), most).astype(held_as)


def setup_inputs(seed: int = 0) -> dict:
    key_of = jax.random.split(jax.random.key(seed), 6)
    samples = centred(key_of[0], (4, TIMES, PANELS), 1.0, 6.0, ((1, 16), (2, 16)))
    panel_geom = draw_panel_geom(jax.random.fold_in(key_of[5], 71), 0)
    panel_slot = jax.vmap(lambda own: jax.random.permutation(own, PAN_OBS))(jax.random.split(key_of[2], N_OBS)).reshape((N_OBS, PAN_OBS)).astype(jnp.int32)
    observer_pos = draw_observer_pos(jax.random.fold_in(key_of[5], 71), 0)
    observer_slot = jax.vmap(lambda own: jax.random.permutation(own, OBS_DEV))(jax.random.split(key_of[4], N_OBS)).reshape((N_OBS, OBS_DEV)).astype(jnp.int32)
    return dict(samples=samples, panel_geom=panel_geom, panel_slot=panel_slot, observer_pos=observer_pos, observer_slot=observer_slot)


def dft_table(window, count):
    step_index = jnp.arange(window, dtype=jnp.int32)
    bin_index = jnp.arange(1, count + 1, dtype=jnp.int32)
    residue = bin_index[:, None] * step_index[None, :] % window
    angles = 2.0 * math.pi / window * residue.astype(jnp.float32)
    hann_window = 0.5 - 0.5 * jnp.cos(2.0 * math.pi / window * step_index.astype(jnp.float32))
    norm_factor = 1.0 / jnp.sqrt(jnp.sum(hann_window * hann_window))
    weighted = hann_window[None, :] * norm_factor
    return jnp.concatenate([jnp.cos(angles) * weighted, -jnp.sin(angles) * weighted], 0).astype(jnp.bfloat16)

def green_tile(listeners, geometry, wavenumber, scale):
    delta = listeners[:, :, None] - geometry[:3, None, :]
    distance = jnp.sqrt(lax.optimization_barrier(jnp.sum(delta * delta, axis=0)))
    inverse = 1.0 / distance
    direction = delta * inverse
    weights = geometry[3][None, :] * scale
    wave_col = wavenumber[:, None, None]
    phases = wave_col * distance
    green_re = jnp.cos(phases) * inverse * (0.25 / math.pi)
    green_im = -jnp.sin(phases) * inverse * (0.25 / math.pi)
    mono_re = wave_col * green_im * weights
    mono_im = -wave_col * green_re * weights
    dip_re = (green_re * inverse - wave_col * green_im) * weights
    dip_im = (green_im * inverse + wave_col * green_re) * weights
    pieces = [jnp.stack([mono_re, mono_im], 2)]
    for axis_id in range(3):
        pieces.append(jnp.stack([dip_re * direction[axis_id], dip_im * direction[axis_id]], 2))
    return jnp.stack(pieces, 2).astype(jnp.bfloat16)

def source_sides(spectra):
    real_part = spectra[0]
    imag_part = spectra[1]
    first = jnp.stack([real_part, -imag_part], 2)
    second = jnp.stack([imag_part, real_part], 2)
    return jnp.stack([first, second], 1)

def reference(samples, panel_geom, panel_slot, observer_pos, observer_slot):
    channels = samples.shape[0]
    table = dft_table(WIN, FREQS)
    records = samples.astype(jnp.float32).reshape(channels, SEGS, WIN, PANELS)
    spectra = jnp.einsum('qw,cgwp->qcgp', table.astype(jnp.float32), records, precision=lax.Precision.HIGHEST)
    spectra = spectra.reshape(2, FREQS, channels, SEGS, PANELS).astype(jnp.bfloat16)
    panel_cols = (panel_slot + (jnp.arange(N_OBS, dtype=jnp.int32) * PAN_OBS)[:, None]).reshape(-1).astype(jnp.int32)
    geometry = jnp.take(panel_geom, panel_cols, axis=1)
    observer_cols = (observer_slot + (jnp.arange(N_OBS, dtype=jnp.int32) * OBS_DEV)[:, None]).reshape(-1).astype(jnp.int32)
    listeners = jnp.take(observer_pos, observer_cols, axis=1)
    wavenumber = 0.25 * jnp.arange(1, FREQS + 1, dtype=jnp.int32).astype(jnp.float32)
    scale = 1.0 / math.sqrt(PANELS)
    spec_blocks = jnp.moveaxis(spectra.reshape(2, FREQS, channels, SEGS, N_OBS, PAN_OBS), 4, 0)
    geom_blocks = jnp.moveaxis(geometry.reshape(4, N_OBS, PAN_OBS), 1, 0)

    def per_block(running, block):
        spec_block, geom_block = block

        def per_bin(item):
            wave_value, spec_bin = item
            tile = green_tile(listeners, geom_block, wave_value[None], scale).astype(jnp.float32)
            sides = source_sides(spec_bin[:, None]).astype(jnp.float32)
            return jnp.einsum('focxp,fzcxgp->ozg', tile, sides, precision=lax.Precision.HIGHEST)
        by_bin = lax.map(per_bin, (wavenumber, jnp.moveaxis(spec_block, 1, 0)))
        return (running + jnp.moveaxis(by_bin, 0, 1), None)
    start_value = jnp.zeros((OBSERVERS, FREQS, 2, SEGS), jnp.float32)
    pressure, _ = lax.scan(per_block, start_value, (spec_blocks, geom_blocks))
    return pressure
```

```python
import functools
import math

import jax
import jax.numpy as jnp
import numpy as np
from jax import lax
from jax.experimental import pallas as pl
from jax.experimental.pallas import tpu as pltpu
from jax.sharding import PartitionSpec as P

WIN = 128
FREQS = 64
NF = 16
NO = 16
BINS = 4
PAN = 512
OBS = 256
CH = 4
HOLD = 4
ROWS = 6 * PAN
SUB = 16
F32 = jnp.float32
BF16 = jnp.bfloat16
MESH = pl.DeviceIdType.MESH

SIN_POLY = (4.4428797, -7.3078165, 3.5977743, -0.7911994)
COS_POLY = (1.414204, -6.9776373, 5.715188, -1.7282139)
STEP_POLY = (9.9999994e-01, -3.1249965e-02, 1.6275267e-04, -3.3845342e-07, 3.5696468e-10)


def dft_table():
    steps = np.arange(WIN, dtype=np.int32)
    bins = np.arange(1, FREQS + 1, dtype=np.int32)
    angles = np.float32(2.0 * math.pi / WIN) * (bins[:, None] * steps[None, :] % WIN).astype(np.float32)
    hann = np.float32(0.5) - np.float32(0.5) * np.cos(np.float32(2.0 * math.pi / WIN) * steps.astype(np.float32))
    weighted = hann[None, :] * (np.float32(1.0) / np.sqrt(np.sum(hann * hann)))
    parts = np.stack([np.cos(angles) * weighted, -np.sin(angles) * weighted], 1)
    return parts.reshape(2 * FREQS, WIN).astype(jnp.bfloat16)


def poly(coefs, x):
    total = coefs[-1] * x + coefs[-2]
    for coef in coefs[-3::-1]:
        total = total * x + coef
    return total


def pieces(x):
    first = x.astype(BF16).astype(F32)
    rest = x - first
    second = rest.astype(BF16).astype(F32)
    return first, second, (rest - second).astype(BF16).astype(F32)


def permuted(array, slot):
    n = array.shape[1]
    hot = (lax.broadcasted_iota(jnp.int32, (n, n), 0) == slot).astype(F32).astype(BF16)
    stacked = jnp.concatenate(pieces(array), 0).astype(BF16)
    picked = jnp.dot(stacked, hot, preferred_element_type=F32)
    return picked[0:8] + picked[8:16] + picked[16:24]


def tile_part(d2, kappa):
    inverse = lax.rsqrt(d2)
    distance = d2 * inverse
    turns = distance * kappa
    turns = turns - ((turns + 12582912.0) - 12582912.0)
    square = turns * turns
    sine = turns * poly(SIN_POLY, square)
    cosine = poly(COS_POLY, square)
    amp = inverse * inverse
    scaled = amp * sine
    c1 = amp - scaled * sine
    s1 = scaled * cosine
    step_cos = poly(STEP_POLY, d2)
    rest = 1.0 - step_cos * step_cos
    step_sin = rest * lax.rsqrt(rest)
    cc, ss, sc, cs = c1 * step_cos, s1 * step_sin, s1 * step_cos, c1 * step_sin
    c0, c2 = cc + ss, cc - ss
    s0, s2 = sc - cs, sc + cs
    twice = step_cos + step_cos
    c3 = twice * c2 - c1
    s3 = twice * s2 - s1
    return ((c0, s0), (c1, s1), (c2, s2), (c3, s3)), inverse, distance


def generate(store, k, quarter, d2_ref, parity, kappa):
    def one(sub, carry):
        base = pl.multiple_of(quarter * 128 + sub * SUB, SUB)
        d2 = d2_ref[parity, pl.ds(pl.multiple_of(sub * SUB, SUB), SUB), :]
        factors, inverse, distance = tile_part(d2, kappa)
        inverse, distance = inverse.astype(BF16), distance.astype(BF16)
        for f in range(BINS):
            c, s = factors[f][0].astype(BF16), factors[f][1].astype(BF16)
            for at, part in enumerate((c, s, c * inverse, s * inverse, c * distance, s * distance)):
                store[k, f, pl.ds(pl.multiple_of(base + at * PAN, SUB), SUB), :] = part
        return carry

    lax.fori_loop(0, 128 // SUB, one, 0, unroll=True)


def contract(store, k, f, le_ref, lm_ref, place_ref, block):
    out = jnp.dot(le_ref[f], store[k, f, 0 : 4 * PAN, :], preferred_element_type=F32)
    mono = jnp.dot(lm_ref[f], store[k, f, 4 * PAN : 6 * PAN, :], preferred_element_type=F32)
    place = place_ref[block]
    return (
        out[0:32] * place[0:1]
        + out[32:64] * place[1:2]
        + out[64:96] * place[2:3]
        + (out[96:128] + mono)
    )


def kernel(
    table_ref,
    samples_ref,
    geom_ref,
    slot_ref,
    pos_ref,
    pos_slot_ref,
    out_ref,
    eight,
    geometry,
    left,
    place_in,
    right,
    d2_ref,
    spec_out,
    spec_in,
    perm,
    le_ref,
    lm_ref,
    store_a,
    store_b,
    part_out,
    part_in,
    place_send,
    place_recv,
    spec_send,
    spec_recv,
    part_send,
    part_recv,
):
    q = lax.axis_index("freq")
    me = lax.axis_index("obs")

    barrier = pltpu.get_barrier_semaphore()

    def greet(step, carry):
        pl.semaphore_signal(barrier, inc=1, device_id=(q, lax.rem(me + step, NO)), device_id_type=MESH)
        pl.semaphore_signal(barrier, inc=1, device_id=(lax.rem(q + step, NF), me), device_id_type=MESH)
        return carry

    lax.fori_loop(1, NO, greet, 0)

    eight[...] = jnp.zeros_like(eight)
    eight[0:3, 0:OBS] = pos_ref[...]
    seen = permuted(eight[:, 0:OBS], pos_slot_ref[...])
    place_in[0] = seen
    place_in[0, 3:4, :] = seen[0:1] * seen[0:1] + seen[1:2] * seen[1:2] + seen[2:3] * seen[2:3]
    place_in[0, 4:5, :] = jnp.ones((1, OBS), F32)

    pl.semaphore_wait(barrier, NO - 1 + NF - 1)

    def place_copy(step):
        return pltpu.make_async_remote_copy(
            src_ref=place_in.at[0],
            dst_ref=place_in.at[NO - step],
            send_sem=place_send.at[step],
            recv_sem=place_recv.at[NO - step],
            device_id=(q, lax.rem(me + step, NO)),
            device_id_type=MESH,
        )

    def spec_copy(step):
        owner = lax.rem(q + step, NF)
        return pltpu.make_async_remote_copy(
            src_ref=spec_out.at[owner],
            dst_ref=spec_in.at[q],
            send_sem=spec_send.at[step],
            recv_sem=spec_recv.at[NF - step],
            device_id=(owner, me),
            device_id_type=MESH,
        )

    def part_copy(step):
        return pltpu.make_async_remote_copy(
            src_ref=part_out.at[step],
            dst_ref=part_in.at[NO - step],
            send_sem=part_send.at[step],
            recv_sem=part_recv.at[NO - step],
            device_id=(q, lax.rem(me + step, NO)),
            device_id_type=MESH,
        )

    def start_all(copy):
        def one(step, carry):
            copy(step).start()
            return carry

        lax.fori_loop(1, NO, one, 0)

    start_all(place_copy)

    for c in range(0, CH, 2):
        pair = [
            jnp.dot(table_ref[...], samples_ref[c + d], preferred_element_type=F32).reshape(NF, 2 * BINS, PAN)
            for d in range(2)
        ]
        spec_out[:, c * 8 : c * 8 + 16, :] = jnp.concatenate(pair, 1).astype(BF16)
    start_all(spec_copy)
    spec_in[q] = spec_out[q]

    eight[...] = jnp.zeros_like(eight)
    eight[0:4, :] = geom_ref[...]
    geometry[...] = permuted(eight[...], slot_ref[...])
    geo = geometry[...]
    eight[0:3, :] = -2.0 * geo[0:3]
    eight[3:4, :] = jnp.ones((1, PAN), F32)
    eight[4:5, :] = geo[0:1] * geo[0:1] + geo[1:2] * geo[1:2] + geo[2:3] * geo[2:3]
    one, two, three = pieces(eight[...])
    side = jnp.concatenate([one, two, one, three, two, one, jnp.zeros((80, PAN), F32)], 0)
    left[...] = side.T.astype(BF16)

    def spread(block):
        one, two, three = pieces(place_in[block])
        right[block] = jnp.concatenate([one, one, two, one, two, three, jnp.zeros((80, OBS), F32)], 0).astype(BF16)

    def distances(turn):
        block, quarter = turn // 4, lax.rem(turn, 4)
        d2_ref[lax.rem(turn, 2)] = jnp.dot(
            left[pl.ds(pl.multiple_of(quarter * 128, 128), 128), :], right[block], preferred_element_type=F32
        )

    kappa = (q.astype(F32) + 0.5) * (0.5 / math.pi)

    def run(gen_store, gen_first, mm_store, mm_first, count):
        def block_step(k, carry):
            def quarter_step(h, inner):
                if mm_store is not None:
                    block = mm_first + k
                    result = contract(mm_store, k, h, le_ref, lm_ref, place_in, block)
                    part_out[block, pl.ds(pl.multiple_of(h * 32, 32), 32), :] = result.astype(BF16)
                if gen_store is not None:
                    turn = (gen_first + k) * 4 + h
                    generate(gen_store, k, h, d2_ref, lax.rem(turn, 2), kappa)
                    distances(jnp.minimum(turn + 1, 4 * NO - 1))
                return inner

            lax.fori_loop(0, 4, quarter_step, 0)
            if mm_store is not None:
                block = mm_first + k

                @pl.when(block > 0)
                def _():
                    part_copy(block).start()

            return carry

        lax.fori_loop(0, count, block_step, 0)

    spread(0)
    distances(jnp.int32(0))

    row = lax.broadcasted_iota(jnp.int32, (PAN, PAN), 0)
    col = lax.broadcasted_iota(jnp.int32, (PAN, PAN), 1)
    source = (row & 15) * 32 + ((row >> 5) & 3) * 8 + (row >> 7) * 2 + ((row >> 4) & 1)
    perm[...] = (source == col).astype(F32).astype(BF16)

    def await_place(step, carry):
        place_copy(step).wait_send()
        place_copy(NO - step).wait_recv()
        spread(step)
        return carry

    lax.fori_loop(1, NO, await_place, 0)
    run(store_a, 0, None, 0, HOLD)

    def await_spec(step, carry):
        spec_copy(step).wait_send()
        spec_copy(NF - step).wait_recv()
        return carry

    lax.fori_loop(1, NF, await_spec, 0)

    geo = geometry[...]
    weight = geo[3:4] * (0.25 / math.pi / math.sqrt(PAN * NO))
    everything = spec_in[...].reshape(PAN, PAN)
    for f in range(BINS):
        wave = (q * BINS + (f + 1)).astype(F32) * 0.25
        rows = jnp.dot(perm[f * 128 : f * 128 + 128, :], everything, preferred_element_type=F32) * weight
        mono, load = rows[0:32], [rows[32 * j + 32 : 32 * j + 64] for j in range(3)]
        load.append(-(load[0] * geo[0:1] + load[1] * geo[1:2] + load[2] * geo[2:3]))
        plain = jnp.concatenate(load, 0)
        turned = jnp.concatenate([x for part in load for x in (-part[16:32], part[0:16])], 0)
        mono_turned = jnp.concatenate([-mono[16:32], mono[0:16]], 0)
        le_ref[f, :, 0:PAN] = (turned * wave).astype(BF16)
        le_ref[f, :, PAN : 2 * PAN] = (plain * wave).astype(BF16)
        le_ref[f, :, 2 * PAN : 3 * PAN] = plain.astype(BF16)
        le_ref[f, :, 3 * PAN : 4 * PAN] = (-turned).astype(BF16)
        lm_ref[f, :, 0:PAN] = (mono_turned * -wave).astype(BF16)
        lm_ref[f, :, PAN : 2 * PAN] = (mono * -wave).astype(BF16)

    rounds = NO // HOLD

    def both(t, carry):
        run(store_b, (2 * t + 1) * HOLD, store_a, 2 * t * HOLD, HOLD)
        run(store_a, (2 * t + 2) * HOLD, store_b, (2 * t + 1) * HOLD, HOLD)
        return carry

    lax.fori_loop(0, rounds // 2 - 1, both, 0)
    run(store_b, (rounds - 1) * HOLD, store_a, (rounds - 2) * HOLD, HOLD)
    run(None, 0, store_b, (rounds - 1) * HOLD, HOLD)

    out_ref[...] = part_out[0].astype(F32)

    def finish(step, carry):
        part_copy(step).wait_send()
        part_copy(NO - step).wait_recv()
        out_ref[...] += part_in[step].astype(F32)
        return carry

    lax.fori_loop(1, NO, finish, 0)


def local(samples, panel_geom, panel_slot, observer_pos, observer_slot):
    vmem = pl.BlockSpec(memory_space=pltpu.VMEM)
    dma = pltpu.SemaphoreType.DMA
    out = pl.pallas_call(
        kernel,
        out_shape=jax.ShapeDtypeStruct((BINS * 2 * NF, OBS), F32),
        in_specs=[vmem] * 6,
        out_specs=vmem,
        scratch_shapes=[
            pltpu.VMEM((8, PAN), F32),
            pltpu.VMEM((8, PAN), F32),
            pltpu.VMEM((PAN, 128), BF16),
            pltpu.VMEM((NO, 8, OBS), F32),
            pltpu.VMEM((NO, 128, OBS), BF16),
            pltpu.VMEM((2, 128, OBS), F32),
            pltpu.VMEM((NF, 32, PAN), BF16),
            pltpu.VMEM((NF, 32, PAN), BF16),
            pltpu.VMEM((PAN, PAN), BF16),
            pltpu.VMEM((BINS, 128, 4 * PAN), BF16),
            pltpu.VMEM((BINS, 32, 2 * PAN), BF16),
            pltpu.VMEM((HOLD, BINS, ROWS, OBS), BF16),
            pltpu.VMEM((HOLD, BINS, ROWS, OBS), BF16),
            pltpu.VMEM((NO, 128, OBS), BF16),
            pltpu.VMEM((NO, 128, OBS), BF16),
            dma((NO,)),
            dma((NO,)),
            dma((NF,)),
            dma((NF,)),
            dma((NO,)),
            dma((NO,)),
        ],
        compiler_params=pltpu.CompilerParams(
            collective_id=0, has_side_effects=True, vmem_limit_bytes=60 * 2**20
        ),
    )(jnp.asarray(dft_table()), samples, panel_geom, panel_slot, observer_pos, observer_slot)
    return out.reshape(BINS, 2, NF, OBS).transpose(3, 0, 1, 2)


def solution(mesh):
    placed = (
        P(None, "freq", "obs"),
        P(None, "obs"),
        P("obs", None),
        P(None, "obs"),
        P("obs", None),
    )
    return jax.shard_map(
        local, mesh=mesh, in_specs=placed, out_specs=P("obs", "freq", None, None), check_vma=False
    )
```

```python
import functools
import math

import jax
import jax.numpy as jnp
import numpy as np
from jax import lax
from jax.experimental import pallas as pl
from jax.experimental.pallas import tpu as pltpu
from jax.sharding import PartitionSpec as P

WIN = 128
FREQS = 64
NF = 16
NO = 16
BINS = 4
PAN = 512
OBS = 256
CH = 4
HELD = 8
ROWS = 4 * PAN
GROUPS = 160
SUB = 16
F32 = jnp.float32
BF16 = jnp.bfloat16
MESH = pl.DeviceIdType.MESH

SIN_POLY = (4.4428797, -7.3078165, 3.5977743, -0.7911994)
COS_POLY = (1.414204, -6.9776373, 5.715188, -1.7282139)
STEP_POLY = (9.9999505e-01, -3.1246377e-02, 1.6224394e-04, -3.1450108e-07)


def dft_table():
    steps = np.arange(WIN, dtype=np.int32)
    bins = np.arange(1, FREQS + 1, dtype=np.int32)
    angles = np.float32(2.0 * math.pi / WIN) * (bins[:, None] * steps[None, :] % WIN).astype(np.float32)
    hann = np.float32(0.5) - np.float32(0.5) * np.cos(np.float32(2.0 * math.pi / WIN) * steps.astype(np.float32))
    weighted = hann[None, :] * (np.float32(1.0) / np.sqrt(np.sum(hann * hann)))
    parts = np.stack([np.cos(angles) * weighted, -np.sin(angles) * weighted], 1)
    return parts.reshape(2 * FREQS, WIN).astype(jnp.bfloat16)


def poly(coefs, x):
    total = coefs[-1] * x + coefs[-2]
    for coef in coefs[-3::-1]:
        total = total * x + coef
    return total


def pieces(x):
    first = x.astype(BF16).astype(F32)
    rest = x - first
    second = rest.astype(BF16).astype(F32)
    return first, second, (rest - second).astype(BF16).astype(F32)


def permuted(array, slot):
    n = array.shape[1]
    hot = (lax.broadcasted_iota(jnp.int32, (n, n), 0) == slot).astype(F32).astype(BF16)
    stacked = jnp.concatenate(pieces(array), 0).astype(BF16)
    picked = jnp.dot(stacked, hot, preferred_element_type=F32)
    return picked[0:8] + picked[8:16] + picked[16:24]


def norm(rows):
    return rows[0:1] * rows[0:1] + rows[1:2] * rows[1:2] + rows[2:3] * rows[2:3]


def tile_part(d2, step_poly):
    inverse = lax.rsqrt(d2)
    turns = d2 * inverse
    turns = turns - ((turns + 12582912.0) - 12582912.0)
    square = turns * turns
    sine = turns * poly(SIN_POLY, square)
    cosine = poly(COS_POLY, square)
    amp = inverse * inverse
    scaled = amp * sine
    c1 = amp - scaled * sine
    s1 = scaled * cosine
    step_cos = poly(step_poly, d2)
    rest = 1.0 - step_cos * step_cos
    step_sin = rest * lax.rsqrt(rest)
    cc, ss, sc, cs = c1 * step_cos, s1 * step_sin, s1 * step_cos, c1 * step_sin
    c0, c2 = cc + ss, cc - ss
    s0, s2 = sc - cs, sc + cs
    twice = step_cos + step_cos
    c3 = twice * c2 - c1
    s3 = twice * s2 - s1
    return ((c0, s0), (c1, s1), (c2, s2), (c3, s3)), inverse


def generate(store, k, quarter, d2_ref, step_poly):
    def one(sub, carry):
        base = pl.multiple_of(quarter * 128 + sub * SUB, SUB)
        d2 = d2_ref[pl.ds(pl.multiple_of(sub * SUB, SUB), SUB), :]
        factors, inverse = tile_part(d2, step_poly)
        for f in range(BINS):
            c, s = factors[f]
            for at, part in enumerate((c, s, c * inverse, s * inverse)):
                store[k, f, pl.ds(pl.multiple_of(base + at * PAN, SUB), SUB), :] = part.astype(BF16)
        return carry

    lax.fori_loop(0, 128 // SUB, one, 0, unroll=True)


def contract(store, k, f, rhs_ref, place_ref, block):
    out = jnp.dot(rhs_ref[f], store[k, f], preferred_element_type=F32)
    place = place_ref[block]
    return (
        out[0:32] * place[0:1]
        + out[32:64] * place[1:2]
        + out[64:96] * place[2:3]
        + out[96:128]
        + out[128:160] * place[3:4]
    )


def kernel(
    table_ref,
    samples_ref,
    geom_ref,
    slot_ref,
    pos_ref,
    pos_slot_ref,
    out_ref,
    eight,
    geometry,
    left,
    place_in,
    place,
    right,
    d2_a,
    d2_b,
    spec_out,
    spec_in,
    perm,
    rhs_ref,
    store_a,
    store_b,
    part_out,
    part_in,
    place_send,
    place_recv,
    spec_send,
    spec_recv,
    part_send,
    part_recv,
):
    q = lax.axis_index("freq")
    me = lax.axis_index("obs")

    barrier = pltpu.get_barrier_semaphore()

    def greet(step, carry):
        pl.semaphore_signal(barrier, inc=1, device_id=(q, lax.rem(me + step, NO)), device_id_type=MESH)
        pl.semaphore_signal(barrier, inc=1, device_id=(lax.rem(q + step, NF), me), device_id_type=MESH)
        return carry

    lax.fori_loop(1, NO, greet, 0)

    eight[...] = jnp.zeros_like(eight)
    eight[0:3, 0:OBS] = pos_ref[...]
    seen = permuted(eight[:, 0:OBS], pos_slot_ref[...])
    place_in[0] = seen

    pl.semaphore_wait(barrier, NO - 1 + NF - 1)

    def place_copy(step):
        return pltpu.make_async_remote_copy(
            src_ref=place_in.at[0],
            dst_ref=place_in.at[NO - step],
            send_sem=place_send.at[step],
            recv_sem=place_recv.at[NO - step],
            device_id=(q, lax.rem(me + step, NO)),
            device_id_type=MESH,
        )

    def spec_copy(step):
        owner = lax.rem(q + step, NF)
        return pltpu.make_async_remote_copy(
            src_ref=spec_out.at[owner],
            dst_ref=spec_in.at[q],
            send_sem=spec_send.at[step],
            recv_sem=spec_recv.at[NF - step],
            device_id=(owner, me),
            device_id_type=MESH,
        )

    def part_copy(step):
        return pltpu.make_async_remote_copy(
            src_ref=part_out.at[step],
            dst_ref=part_in.at[NO - step],
            send_sem=part_send.at[step],
            recv_sem=part_recv.at[NO - step],
            device_id=(q, lax.rem(me + step, NO)),
            device_id_type=MESH,
        )

    def start_all(copy):
        def one(step, carry):
            copy(step).start()
            return carry

        lax.fori_loop(1, NO, one, 0)

    start_all(place_copy)

    for c in range(0, CH, 2):
        pair = [
            jnp.dot(table_ref[...], samples_ref[c + d], preferred_element_type=F32).reshape(NF, 2 * BINS, PAN)
            for d in range(2)
        ]
        spec_out[:, c * 8 : c * 8 + 16, :] = jnp.concatenate(pair, 1).astype(BF16)
    start_all(spec_copy)
    spec_in[q] = spec_out[q]

    eight[...] = jnp.zeros_like(eight)
    eight[0:4, :] = geom_ref[...]
    geometry[...] = permuted(eight[...], slot_ref[...])
    kappa = (q.astype(F32) + 0.5) * (0.5 / math.pi)
    scale = jnp.full((8, 1), kappa, F32)
    middle = jnp.sum(geometry[...], 1, keepdims=True) * (1.0 / PAN)
    geometry[0:3, :] = (geometry[0:3, :] - middle[0:3]) * scale[0:3]
    geo = geometry[...]
    eight[0:3, :] = -2.0 * geo[0:3]
    eight[3:4, :] = jnp.ones((1, PAN), F32)
    eight[4:5, :] = norm(geo)
    one, two, three = pieces(eight[...])
    side = jnp.concatenate([one, two, one, three, two, one, jnp.zeros((80, PAN), F32)], 0)
    left[...] = side.T.astype(BF16)

    def spread(block):
        seen = (place_in[block] - middle) * scale
        place[block] = seen
        place[block, 3:4, :] = norm(seen)
        place[block, 4:5, :] = jnp.ones((1, OBS), F32)
        one, two, three = pieces(place[block])
        right[block] = jnp.concatenate([one, one, two, one, two, three, jnp.zeros((80, OBS), F32)], 0).astype(BF16)

    def block_at(turn):
        return lax.rem(turn + 1, NO)

    def distances(turn, d2_ref):
        block, quarter = block_at(turn // 4), lax.rem(turn, 4)
        d2_ref[...] = jnp.dot(
            left[pl.ds(pl.multiple_of(quarter * 128, 128), 128), :], right[block], preferred_element_type=F32
        )

    inverse_square = 1.0 / (kappa * kappa)
    step_poly = [jnp.float32(STEP_POLY[0])]
    power = jnp.float32(1.0)
    for coef in STEP_POLY[1:]:
        power = power * inverse_square
        step_poly.append(coef * power)

    def run(count, gen_store=None, gen_slot=0, gen_turn=0, mm_store=None, mm_turn=0, mm_count=1):
        def block_step(k, carry):
            def half_step(half, inner):
                for h in range(2):
                    f = half * 2 + h
                    if mm_store is not None:
                        for m in range(mm_count):
                            slot = k * mm_count + m
                            block = block_at(mm_turn + slot)
                            result = contract(mm_store, slot, f, rhs_ref, place, block)
                            part_out[block, pl.ds(pl.multiple_of(f * 32, 32), 32), :] = result.astype(BF16)
                    if gen_store is not None:
                        turn = (gen_turn + k) * 4 + f
                        distances(jnp.minimum(turn + 1, 4 * NO - 1), (d2_b, d2_a)[h])
                        generate(gen_store, gen_slot + k, f, (d2_a, d2_b)[h], step_poly)
                return inner

            lax.fori_loop(0, 2, half_step, 0)
            if mm_store is not None and mm_turn < NO - 1:
                for m in range(mm_count):
                    part_copy(block_at(mm_turn + k * mm_count + m)).start()
            return carry

        lax.fori_loop(0, count, block_step, 0)

    spread(0)

    row = lax.broadcasted_iota(jnp.int32, (PAN, PAN), 0)
    col = lax.broadcasted_iota(jnp.int32, (PAN, PAN), 1)
    source = (row & 15) * 32 + ((row >> 5) & 3) * 8 + (row >> 7) * 2 + ((row >> 4) & 1)
    perm[...] = (source == col).astype(F32).astype(BF16)

    def await_place(step, carry):
        place_copy(step).wait_send()
        place_copy(NO - step).wait_recv()
        spread(step)
        return carry

    lax.fori_loop(1, NO, await_place, 0)
    distances(jnp.int32(0), d2_a)
    run(HELD, store_a)

    def await_spec(step, carry):
        spec_copy(step).wait_send()
        spec_copy(NF - step).wait_recv()
        return carry

    lax.fori_loop(1, NF, await_spec, 0)

    def turned(x):
        return jnp.concatenate([-x[16:32], x[0:16]], 0)

    geo = geometry[...]
    weight = geo[3:4] * (0.25 / math.pi / math.sqrt(PAN * NO)) * (kappa * kappa)
    square = norm(geo)
    everything = spec_in[...].reshape(PAN, PAN)
    for f in range(BINS):
        wave = (q * BINS + (f + 1)).astype(F32) * 0.25 / kappa
        rows = jnp.dot(perm[f * 128 : f * 128 + 128, :], everything, preferred_element_type=F32) * weight
        mono = turned(rows[0:32]) * wave
        load = [rows[32 * j + 32 : 32 * j + 64] for j in range(3)]
        load.append(-(load[0] * geo[0:1] + load[1] * geo[1:2] + load[2] * geo[2:3]))
        near = [load[j] + mono * (2.0 * geo[j : j + 1]) for j in range(3)] + [load[3] - mono * square, -mono]
        far = [turned(x) * wave for x in load] + [jnp.zeros((32, PAN), F32)]
        for at, side in enumerate((far, near)):
            rhs_ref[f, :, 2 * at * PAN : (2 * at + 1) * PAN] = jnp.concatenate(side, 0).astype(BF16)
            rhs_ref[f, :, (2 * at + 1) * PAN : (2 * at + 2) * PAN] = jnp.concatenate(
                [-turned(x) for x in side], 0
            ).astype(BF16)

    run(4, store_b, 0, 8, store_a, 0, 2)
    run(2, store_a, 0, 12, store_b, 8, 2)
    run(1, store_b, 0, 14, store_a, 12, 2)
    run(1, store_a, 0, 15, store_b, 14, 1)
    run(1, mm_store=store_a, mm_turn=15)

    out_ref[...] = part_out[0].astype(F32)

    def finish(step, carry):
        part_copy(step).wait_send()
        part_copy(NO - step).wait_recv()
        out_ref[...] += part_in[step].astype(F32)
        return carry

    lax.fori_loop(1, NO, finish, 0)


def local(samples, panel_geom, panel_slot, observer_pos, observer_slot):
    vmem = pl.BlockSpec(memory_space=pltpu.VMEM)
    dma = pltpu.SemaphoreType.DMA
    out = pl.pallas_call(
        kernel,
        out_shape=jax.ShapeDtypeStruct((BINS * 2 * NF, OBS), F32),
        in_specs=[vmem] * 6,
        out_specs=vmem,
        scratch_shapes=[
            pltpu.VMEM((8, PAN), F32),
            pltpu.VMEM((8, PAN), F32),
            pltpu.VMEM((PAN, 128), BF16),
            pltpu.VMEM((NO, 8, OBS), F32),
            pltpu.VMEM((NO, 8, OBS), F32),
            pltpu.VMEM((NO, 128, OBS), BF16),
            pltpu.VMEM((128, OBS), F32),
            pltpu.VMEM((128, OBS), F32),
            pltpu.VMEM((NF, 32, PAN), BF16),
            pltpu.VMEM((NF, 32, PAN), BF16),
            pltpu.VMEM((PAN, PAN), BF16),
            pltpu.VMEM((BINS, GROUPS, ROWS), BF16),
            pltpu.VMEM((HELD, BINS, ROWS, OBS), BF16),
            pltpu.VMEM((HELD // 2, BINS, ROWS, OBS), BF16),
            pltpu.VMEM((NO, 128, OBS), BF16),
            pltpu.VMEM((NO, 128, OBS), BF16),
            dma((NO,)),
            dma((NO,)),
            dma((NF,)),
            dma((NF,)),
            dma((NO,)),
            dma((NO,)),
        ],
        compiler_params=pltpu.CompilerParams(
            collective_id=0, has_side_effects=True, vmem_limit_bytes=60 * 2**20
        ),
    )(jnp.asarray(dft_table()), samples, panel_geom, panel_slot, observer_pos, observer_slot)
    return out.reshape(BINS, 2, NF, OBS).transpose(3, 0, 1, 2)


def solution(mesh):
    placed = (
        P(None, "freq", "obs"),
        P(None, "obs"),
        P("obs", None),
        P(None, "obs"),
        P("obs", None),
    )
    return jax.shard_map(
        local, mesh=mesh, in_specs=placed, out_specs=P("obs", "freq", None, None), check_vma=False
    )
```

```python
import functools
import math

import jax
import jax.numpy as jnp
import numpy as np
from jax import lax
from jax.experimental import pallas as pl
from jax.experimental.pallas import tpu as pltpu
from jax.sharding import PartitionSpec as P

WIN = 128
FREQS = 64
NF = 16
NO = 16
BINS = 4
PAN = 512
OBS = 256
CH = 4
HELD = 8
ROWS = 4 * PAN
GROUPS = 160
SUB = 16
F32 = jnp.float32
BF16 = jnp.bfloat16
MESH = pl.DeviceIdType.MESH

SIN_POLY = (4.4428797, -7.3078165, 3.5977743, -0.7911994)
COS_POLY = (1.414204, -6.9776373, 5.715188, -1.7282139)
STEP_POLY = (9.9999505e-01, -3.1246377e-02, 1.6224394e-04, -3.1450108e-07)


def dft_table():
    steps = np.arange(WIN, dtype=np.int32)
    bins = np.arange(1, FREQS + 1, dtype=np.int32)
    angles = np.float32(2.0 * math.pi / WIN) * (bins[:, None] * steps[None, :] % WIN).astype(np.float32)
    hann = np.float32(0.5) - np.float32(0.5) * np.cos(np.float32(2.0 * math.pi / WIN) * steps.astype(np.float32))
    weighted = hann[None, :] * (np.float32(1.0) / np.sqrt(np.sum(hann * hann)))
    parts = np.stack([np.cos(angles) * weighted, -np.sin(angles) * weighted], 1)
    return parts.reshape(2 * FREQS, WIN).astype(jnp.bfloat16)


def poly(coefs, x):
    total = coefs[-1] * x + coefs[-2]
    for coef in coefs[-3::-1]:
        total = total * x + coef
    return total


def pieces(x):
    first = x.astype(BF16).astype(F32)
    rest = x - first
    second = rest.astype(BF16).astype(F32)
    return first, second, (rest - second).astype(BF16).astype(F32)


def permuted(array, slot):
    n = array.shape[1]
    hot = (lax.broadcasted_iota(jnp.int32, (n, n), 0) == slot).astype(F32).astype(BF16)
    stacked = jnp.concatenate(pieces(array), 0).astype(BF16)
    picked = jnp.dot(stacked, hot, preferred_element_type=F32)
    return picked[0:8] + picked[8:16] + picked[16:24]


def norm(rows):
    return rows[0:1] * rows[0:1] + rows[1:2] * rows[1:2] + rows[2:3] * rows[2:3]


def tile_part(d2, step_poly):
    inverse = lax.rsqrt(d2)
    turns = d2 * inverse
    turns = turns - ((turns + 12582912.0) - 12582912.0)
    square = turns * turns
    sine = turns * poly(SIN_POLY, square)
    cosine = poly(COS_POLY, square)
    amp = inverse * inverse
    scaled = amp * sine
    c1 = amp - scaled * sine
    s1 = scaled * cosine
    step_cos = poly(step_poly, d2)
    rest = 1.0 - step_cos * step_cos
    step_sin = rest * lax.rsqrt(rest)
    cc, ss, sc, cs = c1 * step_cos, s1 * step_sin, s1 * step_cos, c1 * step_sin
    c0, c2 = cc + ss, cc - ss
    s0, s2 = sc - cs, sc + cs
    twice = step_cos + step_cos
    c3 = twice * c2 - c1
    s3 = twice * s2 - s1
    return ((c0, s0), (c1, s1), (c2, s2), (c3, s3)), inverse


def generate(store, k, quarter, d2_ref, step_poly):
    def one(sub, carry):
        base = pl.multiple_of(quarter * 128 + sub * SUB, SUB)
        d2 = d2_ref[pl.ds(pl.multiple_of(sub * SUB, SUB), SUB), :]
        factors, inverse = tile_part(d2, step_poly)
        for f in range(BINS):
            c, s = factors[f]
            for at, part in enumerate((c, s, c * inverse, s * inverse)):
                store[k, f, pl.ds(pl.multiple_of(base + at * PAN, SUB), SUB), :] = part.astype(BF16)
        return carry

    lax.fori_loop(0, 128 // SUB, one, 0, unroll=True)


def contract(store, k, f, rhs_ref, place_ref, block):
    out = jnp.dot(rhs_ref[f], store[k, f], preferred_element_type=F32)
    place = place_ref[block]
    return (
        out[0:32] * place[0:1]
        + out[32:64] * place[1:2]
        + out[64:96] * place[2:3]
        + out[96:128]
        + out[128:160] * place[3:4]
    )


def kernel(
    table_ref,
    samples_ref,
    geom_ref,
    slot_ref,
    pos_ref,
    pos_slot_ref,
    out_ref,
    eight,
    geometry,
    left,
    place_in,
    place,
    right,
    d2_a,
    d2_b,
    spec_out,
    spec_in,
    rhs_ref,
    store_a,
    store_b,
    part_out,
    part_in,
    place_send,
    place_recv,
    spec_send,
    spec_recv,
    part_send,
    part_recv,
):
    q = lax.axis_index("freq")
    me = lax.axis_index("obs")

    barrier = pltpu.get_barrier_semaphore()

    def greet(step, carry):
        pl.semaphore_signal(barrier, inc=1, device_id=(q, lax.rem(me + step, NO)), device_id_type=MESH)
        pl.semaphore_signal(barrier, inc=1, device_id=(lax.rem(q + step, NF), me), device_id_type=MESH)
        return carry

    lax.fori_loop(1, NO, greet, 0)

    eight[...] = jnp.zeros_like(eight)
    eight[0:3, 0:OBS] = pos_ref[...]
    seen = permuted(eight[:, 0:OBS], pos_slot_ref[...])
    place_in[0] = seen

    def place_copy(step):
        return pltpu.make_async_remote_copy(
            src_ref=place_in.at[0],
            dst_ref=place_in.at[NO - step],
            send_sem=place_send.at[step],
            recv_sem=place_recv.at[NO - step],
            device_id=(q, lax.rem(me + step, NO)),
            device_id_type=MESH,
        )

    def spec_copy(step):
        owner = lax.rem(q + step, NF)
        return pltpu.make_async_remote_copy(
            src_ref=spec_out.at[owner],
            dst_ref=spec_in.at[q],
            send_sem=spec_send.at[step],
            recv_sem=spec_recv.at[NF - step],
            device_id=(owner, me),
            device_id_type=MESH,
        )

    def part_copy(step):
        return pltpu.make_async_remote_copy(
            src_ref=part_out.at[step],
            dst_ref=part_in.at[NO - step],
            send_sem=part_send.at[step],
            recv_sem=part_recv.at[NO - step],
            device_id=(q, lax.rem(me + step, NO)),
            device_id_type=MESH,
        )

    def start_all(copy):
        def one(step, carry):
            copy(step).start()
            return carry

        lax.fori_loop(1, NO, one, 0)

    for c in range(0, CH, 2):
        pair = [
            jnp.dot(table_ref[...], samples_ref[c + d], preferred_element_type=F32).reshape(NF, 2 * BINS, PAN)
            for d in range(2)
        ]
        spec_out[:, c * 8 : c * 8 + 16, :] = jnp.concatenate(pair, 1).astype(BF16)
    spec_in[q] = spec_out[q]

    eight[...] = jnp.zeros_like(eight)
    eight[0:4, :] = geom_ref[...]
    geometry[...] = permuted(eight[...], slot_ref[...])
    kappa = (q.astype(F32) + 0.5) * (0.5 / math.pi)
    scale = jnp.full((8, 1), kappa, F32)
    middle = jnp.sum(geometry[...], 1, keepdims=True) * (1.0 / PAN)
    geometry[0:3, :] = (geometry[0:3, :] - middle[0:3]) * scale[0:3]
    geo = geometry[...]
    eight[0:3, :] = -2.0 * geo[0:3]
    eight[3:4, :] = jnp.ones((1, PAN), F32)
    eight[4:5, :] = norm(geo)
    one, two, three = pieces(eight[...])
    side = jnp.concatenate([one, two, one, three, two, one, jnp.zeros((80, PAN), F32)], 0)
    left[...] = side.T.astype(BF16)

    def spread(block):
        seen = (place_in[block] - middle) * scale
        place[block] = seen
        place[block, 3:4, :] = norm(seen)
        place[block, 4:5, :] = jnp.ones((1, OBS), F32)
        one, two, three = pieces(place[block])
        right[block] = jnp.concatenate([one, one, two, one, two, three, jnp.zeros((16, OBS), F32)], 0).astype(BF16)

    def distances(turn, d2_ref):
        block, quarter = turn // 4, lax.rem(turn, 4)
        d2_ref[...] = jnp.dot(
            left[pl.ds(pl.multiple_of(quarter * 128, 128), 128), 0:64], right[block], preferred_element_type=F32
        )

    inverse_square = 1.0 / (kappa * kappa)
    step_poly = [jnp.float32(STEP_POLY[0])]
    power = jnp.float32(1.0)
    for coef in STEP_POLY[1:]:
        power = power * inverse_square
        step_poly.append(coef * power)

    def await_place(block):
        place_copy(NO - block).wait_recv()
        spread(block)

    def run(count, gen_store=None, gen_slot=0, gen_block=0, mm_store=None, mm_slot=0, mm_block=0, mm_count=1):
        def block_step(k, carry):
            def half_step(half, inner):
                if mm_store is None and gen_block > 0:
                    @pl.when(half == 1)
                    def _():
                        await_place(gen_block + k + 1)

                for h in range(2):
                    f = half * 2 + h
                    if mm_store is not None:
                        for m in range(mm_count):
                            at = k * mm_count + m
                            result = contract(mm_store, mm_slot + at, f, rhs_ref, place, mm_block + at)
                            part_out[mm_block + at, pl.ds(pl.multiple_of(f * 32, 32), 32), :] = result.astype(BF16)
                    if gen_store is not None:
                        turn = (gen_block + k) * 4 + f
                        distances(jnp.minimum(turn + 1, (gen_block + count) * 4 - 1 if gen_block == 0 else 4 * NO - 1), (d2_b, d2_a)[h])
                        generate(gen_store, gen_slot + k, f, (d2_a, d2_b)[h], step_poly)
                return inner

            lax.fori_loop(0, 2, half_step, 0)
            if mm_store is not None and mm_block > 0:
                for m in range(mm_count):
                    part_copy(mm_block + k * mm_count + m).start()
            return carry

        lax.fori_loop(0, count, block_step, 0)

    spread(0)

    row = lax.broadcasted_iota(jnp.int32, (PAN, PAN), 0)
    col = lax.broadcasted_iota(jnp.int32, (PAN, PAN), 1)
    source = (row & 15) * 32 + ((row >> 5) & 3) * 8 + (row >> 7) * 2 + ((row >> 4) & 1)
    perm = (source == col).astype(F32).astype(BF16)
    for side in range(2):
        store_b[0, side, 0:PAN, :] = perm[:, side * 256 : side * 256 + 256]

    distances(jnp.int32(0), d2_a)
    run(1, store_b, HELD // 2)

    pl.semaphore_wait(barrier, NO - 1 + NF - 1)
    start_all(place_copy)
    start_all(spec_copy)
    await_place(1)
    distances(jnp.int32(4), d2_a)
    run(HELD, store_a, 0, 1)

    def await_rest(step, carry):
        await_place(step)
        return carry

    lax.fori_loop(HELD + 2, NO, await_rest, 0)

    def await_spec(step, carry):
        spec_copy(step).wait_send()
        spec_copy(NF - step).wait_recv()
        return carry

    lax.fori_loop(1, NF, await_spec, 0)

    def turned(x):
        return jnp.concatenate([-x[16:32], x[0:16]], 0)

    geo = geometry[...]
    weight = geo[3:4] * (0.25 / math.pi / math.sqrt(PAN * NO)) * (kappa * kappa)
    square = norm(geo)
    everything = spec_in[...].reshape(PAN, PAN)
    for f in range(BINS):
        wave = (q * BINS + (f + 1)).astype(F32) * 0.25 / kappa
        perm = jnp.concatenate([store_b[0, side, f * 128 : f * 128 + 128, :] for side in range(2)], 1)
        rows = jnp.dot(perm, everything, preferred_element_type=F32) * weight
        mono = turned(rows[0:32]) * wave
        load = [rows[32 * j + 32 : 32 * j + 64] for j in range(3)]
        load.append(-(load[0] * geo[0:1] + load[1] * geo[1:2] + load[2] * geo[2:3]))
        near = [load[j] + mono * (2.0 * geo[j : j + 1]) for j in range(3)] + [load[3] - mono * square, -mono]
        far = [turned(x) * wave for x in load] + [jnp.zeros((32, PAN), F32)]
        for at, side in enumerate((far, near)):
            rhs_ref[f, :, 2 * at * PAN : (2 * at + 1) * PAN] = jnp.concatenate(side, 0).astype(BF16)
            rhs_ref[f, :, (2 * at + 1) * PAN : (2 * at + 2) * PAN] = jnp.concatenate(
                [-turned(x) for x in side], 0
            ).astype(BF16)

    run(4, store_b, 0, 9, store_a, 0, 1, 2)
    run(2, store_a, 0, 13, store_b, 0, 9, 2)
    run(1, store_b, 0, 15, store_a, 0, 13, 2)
    run(1, mm_store=store_b, mm_slot=0, mm_block=15)
    run(1, mm_store=store_b, mm_slot=HELD // 2, mm_block=0)

    out_ref[...] = part_out[0].astype(F32)

    def finish(step, carry):
        place_copy(step).wait_send()
        part_copy(step).wait_send()
        part_copy(NO - step).wait_recv()
        out_ref[...] += part_in[step].astype(F32)
        return carry

    lax.fori_loop(1, NO, finish, 0)


def local(samples, panel_geom, panel_slot, observer_pos, observer_slot):
    vmem = pl.BlockSpec(memory_space=pltpu.VMEM)
    dma = pltpu.SemaphoreType.DMA
    out = pl.pallas_call(
        kernel,
        out_shape=jax.ShapeDtypeStruct((BINS * 2 * NF, OBS), F32),
        in_specs=[vmem] * 6,
        out_specs=vmem,
        scratch_shapes=[
            pltpu.VMEM((8, PAN), F32),
            pltpu.VMEM((8, PAN), F32),
            pltpu.VMEM((PAN, 128), BF16),
            pltpu.VMEM((NO, 8, OBS), F32),
            pltpu.VMEM((NO, 8, OBS), F32),
            pltpu.VMEM((NO, 64, OBS), BF16),
            pltpu.VMEM((128, OBS), F32),
            pltpu.VMEM((128, OBS), F32),
            pltpu.VMEM((NF, 32, PAN), BF16),
            pltpu.VMEM((NF, 32, PAN), BF16),
            pltpu.VMEM((BINS, GROUPS, ROWS), BF16),
            pltpu.VMEM((HELD, BINS, ROWS, OBS), BF16),
            pltpu.VMEM((HELD // 2 + 1, BINS, ROWS, OBS), BF16),
            pltpu.VMEM((NO, 128, OBS), BF16),
            pltpu.VMEM((NO, 128, OBS), BF16),
            dma((NO,)),
            dma((NO,)),
            dma((NF,)),
            dma((NF,)),
            dma((NO,)),
            dma((NO,)),
        ],
        compiler_params=pltpu.CompilerParams(
            collective_id=0, has_side_effects=True, vmem_limit_bytes=63 * 2**20
        ),
    )(jnp.asarray(dft_table()), samples, panel_geom, panel_slot, observer_pos, observer_slot)
    return out.reshape(BINS, 2, NF, OBS).transpose(3, 0, 1, 2)


def solution(mesh):
    placed = (
        P(None, "freq", "obs"),
        P(None, "obs"),
        P("obs", None),
        P(None, "obs"),
        P("obs", None),
    )
    return jax.shard_map(
        local, mesh=mesh, in_specs=placed, out_specs=P("obs", "freq", None, None), check_vma=False
    )
```

```python
import functools
import math

import jax
import jax.numpy as jnp
import numpy as np
from jax import lax
from jax.experimental import pallas as pl
from jax.experimental.pallas import tpu as pltpu
from jax.sharding import PartitionSpec as P

WIN = 128
FREQS = 64
NF = 16
NO = 16
BINS = 4
PAN = 512
OBS = 256
CH = 4
HELD = 8
ROWS = 4 * PAN
GROUPS = 160
SUB = 16
F32 = jnp.float32
BF16 = jnp.bfloat16
MESH = pl.DeviceIdType.MESH

SIN_POLY = (4.4428797, -7.3078165, 3.5977743, -0.7911994)
COS_POLY = (1.414204, -6.9776373, 5.715188, -1.7282139)
STEP_POLY = (9.9999505e-01, -3.1246377e-02, 1.6224394e-04, -3.1450108e-07)


def dft_table():
    steps = np.arange(WIN, dtype=np.int32)
    bins = np.arange(1, FREQS + 1, dtype=np.int32)
    angles = np.float32(2.0 * math.pi / WIN) * (bins[:, None] * steps[None, :] % WIN).astype(np.float32)
    hann = np.float32(0.5) - np.float32(0.5) * np.cos(np.float32(2.0 * math.pi / WIN) * steps.astype(np.float32))
    weighted = hann[None, :] * (np.float32(1.0) / np.sqrt(np.sum(hann * hann)))
    parts = np.stack([np.cos(angles) * weighted, -np.sin(angles) * weighted], 1)
    return parts.reshape(2 * FREQS, WIN).astype(jnp.bfloat16)


def poly(coefs, x):
    total = coefs[-1] * x + coefs[-2]
    for coef in coefs[-3::-1]:
        total = total * x + coef
    return total


def pieces(x):
    first = x.astype(BF16).astype(F32)
    rest = x - first
    second = rest.astype(BF16).astype(F32)
    return first, second, (rest - second).astype(BF16).astype(F32)


def permuted(array, slot):
    n = array.shape[1]
    hot = (lax.broadcasted_iota(jnp.int32, (n, n), 0) == slot).astype(F32).astype(BF16)
    stacked = jnp.concatenate(pieces(array), 0).astype(BF16)
    picked = jnp.dot(stacked, hot, preferred_element_type=F32)
    return picked[0:8] + picked[8:16] + picked[16:24]


def norm(rows):
    return rows[0:1] * rows[0:1] + rows[1:2] * rows[1:2] + rows[2:3] * rows[2:3]


def tile_part(d2, step_poly):
    inverse = lax.rsqrt(d2)
    turns = d2 * inverse
    turns = turns - ((turns + 12582912.0) - 12582912.0)
    square = turns * turns
    sine = turns * poly(SIN_POLY, square)
    cosine = poly(COS_POLY, square)
    amp = inverse * inverse
    scaled = amp * sine
    c1 = amp - scaled * sine
    s1 = scaled * cosine
    step_cos = poly(step_poly, d2)
    rest = 1.0 - step_cos * step_cos
    step_sin = rest * lax.rsqrt(rest)
    cc, ss, sc, cs = c1 * step_cos, s1 * step_sin, s1 * step_cos, c1 * step_sin
    c0, c2 = cc + ss, cc - ss
    s0, s2 = sc - cs, sc + cs
    twice = step_cos + step_cos
    c3 = twice * c2 - c1
    s3 = twice * s2 - s1
    return ((c0, s0), (c1, s1), (c2, s2), (c3, s3)), inverse


def generate(store, k, quarter, d2_ref, step_poly):
    def one(sub, carry):
        base = pl.multiple_of(quarter * 128 + sub * SUB, SUB)
        d2 = d2_ref[pl.ds(pl.multiple_of(sub * SUB, SUB), SUB), :]
        factors, inverse = tile_part(d2, step_poly)
        for f in range(BINS):
            c, s = factors[f]
            for at, part in enumerate((c, s, c * inverse, s * inverse)):
                store[k, f, pl.ds(pl.multiple_of(base + at * PAN, SUB), SUB), :] = part.astype(BF16)
        return carry

    lax.fori_loop(0, 128 // SUB, one, 0, unroll=True)


def contract(store, k, f, rhs_ref, place_ref, block):
    out = jnp.dot(rhs_ref[f], store[k, f], preferred_element_type=F32)
    place = place_ref[block]
    return (
        out[0:32] * place[0:1]
        + out[32:64] * place[1:2]
        + out[64:96] * place[2:3]
        + out[96:128]
        + out[128:160] * place[3:4]
    )


def kernel(
    table_ref,
    samples_ref,
    geom_ref,
    slot_ref,
    pos_ref,
    pos_slot_ref,
    out_ref,
    eight,
    geometry,
    left,
    place_in,
    place,
    right,
    d2_ref,
    spec_out,
    spec_in,
    rhs_ref,
    store_a,
    store_b,
    part_out,
    part_in,
    place_send,
    place_recv,
    spec_send,
    spec_recv,
    part_send,
    part_recv,
):
    q = lax.axis_index("freq")
    me = lax.axis_index("obs")

    barrier = pltpu.get_barrier_semaphore()

    def greet(step, carry):
        pl.semaphore_signal(barrier, inc=1, device_id=(q, lax.rem(me + step, NO)), device_id_type=MESH)
        pl.semaphore_signal(barrier, inc=1, device_id=(lax.rem(q + step, NF), me), device_id_type=MESH)
        return carry

    lax.fori_loop(1, NO, greet, 0)

    eight[...] = jnp.zeros_like(eight)
    eight[0:3, 0:OBS] = pos_ref[...]
    seen = permuted(eight[:, 0:OBS], pos_slot_ref[...])
    place_in[0] = seen

    def place_copy(step):
        return pltpu.make_async_remote_copy(
            src_ref=place_in.at[0],
            dst_ref=place_in.at[NO - step],
            send_sem=place_send.at[step],
            recv_sem=place_recv.at[NO - step],
            device_id=(q, lax.rem(me + step, NO)),
            device_id_type=MESH,
        )

    def spec_copy(step):
        owner = lax.rem(q + step, NF)
        return pltpu.make_async_remote_copy(
            src_ref=spec_out.at[owner],
            dst_ref=spec_in.at[q],
            send_sem=spec_send.at[step],
            recv_sem=spec_recv.at[NF - step],
            device_id=(owner, me),
            device_id_type=MESH,
        )

    def part_copy(step):
        return pltpu.make_async_remote_copy(
            src_ref=part_out.at[step],
            dst_ref=part_in.at[NO - step],
            send_sem=part_send.at[step],
            recv_sem=part_recv.at[NO - step],
            device_id=(q, lax.rem(me + step, NO)),
            device_id_type=MESH,
        )

    def start_all(copy):
        def one(step, carry):
            copy(NO - step).start()
            return carry

        lax.fori_loop(1, NO, one, 0)

    for c in range(0, CH, 2):
        pair = [
            jnp.dot(table_ref[...], samples_ref[c + d], preferred_element_type=F32).reshape(NF, 2 * BINS, PAN)
            for d in range(2)
        ]
        spec_out[:, c * 8 : c * 8 + 16, :] = jnp.concatenate(pair, 1).astype(BF16)
    spec_in[q] = spec_out[q]

    eight[...] = jnp.zeros_like(eight)
    eight[0:4, :] = geom_ref[...]
    geometry[...] = permuted(eight[...], slot_ref[...])
    kappa = (q.astype(F32) + 0.5) * (0.5 / math.pi)
    scale = jnp.full((8, 1), kappa, F32)
    middle = jnp.sum(geometry[...], 1, keepdims=True) * (1.0 / PAN)
    geometry[0:3, :] = (geometry[0:3, :] - middle[0:3]) * scale[0:3]
    geo = geometry[...]
    eight[0:3, :] = -2.0 * geo[0:3]
    eight[3:4, :] = jnp.ones((1, PAN), F32)
    eight[4:5, :] = norm(geo)
    one, two, three = pieces(eight[...])
    side = jnp.concatenate([one, two, one, three, two, one, jnp.zeros((80, PAN), F32)], 0)
    left[...] = side.T.astype(BF16)

    def spread(block):
        seen = (place_in[block] - middle) * scale
        place[block] = seen
        place[block, 3:4, :] = norm(seen)
        place[block, 4:5, :] = jnp.ones((1, OBS), F32)
        one, two, three = pieces(place[block])
        right[block] = jnp.concatenate([one, one, two, one, two, three, jnp.zeros((16, OBS), F32)], 0).astype(BF16)

    def distances(turn):
        block, half = turn // 2, lax.rem(turn, 2)
        d2_ref[...] = jnp.dot(
            left[pl.ds(pl.multiple_of(half * 256, 256), 256), 0:64], right[block], preferred_element_type=F32
        )

    inverse_square = 1.0 / (kappa * kappa)
    step_poly = [jnp.float32(STEP_POLY[0])]
    power = jnp.float32(1.0)
    for coef in STEP_POLY[1:]:
        power = power * inverse_square
        step_poly.append(coef * power)

    def await_place(block):
        place_copy(NO - block).wait_recv()
        spread(block)

    def run(count, gen_store=None, gen_slot=0, gen_block=0, mm_store=None, mm_slot=0, mm_block=0, mm_count=1):
        def block_step(k, carry):
            def half_step(half, inner):
                if mm_store is None and gen_block > 0:
                    @pl.when(half == 1)
                    def _():
                        await_place(gen_block + k + 1)

                for h in range(2):
                    f = half * 2 + h
                    if mm_store is not None:
                        for m in range(mm_count):
                            at = k * mm_count + m
                            result = contract(mm_store, mm_slot + at, f, rhs_ref, place, mm_block + at)
                            part_out[mm_block + at, pl.ds(pl.multiple_of(f * 32, 32), 32), :] = result.astype(BF16)
                    if gen_store is not None:
                        generate(gen_store, gen_slot + k, f, d2_ref.at[h * 128:h * 128 + 128], step_poly)
                if gen_store is not None:
                    turn = (gen_block + k) * 2 + half
                    distances(jnp.minimum(turn + 1, 1 if gen_block == 0 else 2 * NO - 1))
                return inner

            lax.fori_loop(0, 2, half_step, 0)
            if mm_store is not None and mm_block > 0:
                for m in range(mm_count):
                    part_copy(mm_block + k * mm_count + m).start()
            return carry

        lax.fori_loop(0, count, block_step, 0)

    spread(0)

    row = lax.broadcasted_iota(jnp.int32, (PAN, PAN), 0)
    col = lax.broadcasted_iota(jnp.int32, (PAN, PAN), 1)
    source = (row & 15) * 32 + ((row >> 5) & 3) * 8 + (row >> 7) * 2 + ((row >> 4) & 1)
    perm = (source == col).astype(F32).astype(BF16)
    for side in range(2):
        store_b[0, side, 0:PAN, :] = perm[:, side * 256 : side * 256 + 256]

    distances(jnp.int32(0))
    run(1, store_b, HELD // 2)

    pl.semaphore_wait(barrier, NO - 1 + NF - 1)
    start_all(place_copy)
    start_all(spec_copy)
    await_place(1)
    distances(jnp.int32(2))
    run(HELD, store_a, 0, 1)

    def await_rest(step, carry):
        await_place(step)
        return carry

    lax.fori_loop(HELD + 2, NO, await_rest, 0)

    def await_spec(step, carry):
        spec_copy(step).wait_send()
        spec_copy(NF - step).wait_recv()
        return carry

    lax.fori_loop(1, NF, await_spec, 0)

    def turned(x):
        return jnp.concatenate([-x[16:32], x[0:16]], 0)

    geo = geometry[...]
    weight = geo[3:4] * (0.25 / math.pi / math.sqrt(PAN * NO)) * (kappa * kappa)
    square = norm(geo)
    everything = spec_in[...].reshape(PAN, PAN)
    for f in range(BINS):
        wave = (q * BINS + (f + 1)).astype(F32) * 0.25 / kappa
        perm = jnp.concatenate([store_b[0, side, f * 128 : f * 128 + 128, :] for side in range(2)], 1)
        rows = jnp.dot(perm, everything, preferred_element_type=F32) * weight
        mono = turned(rows[0:32]) * wave
        load = [rows[32 * j + 32 : 32 * j + 64] for j in range(3)]
        load.append(-(load[0] * geo[0:1] + load[1] * geo[1:2] + load[2] * geo[2:3]))
        near = [load[j] + mono * (2.0 * geo[j : j + 1]) for j in range(3)] + [load[3] - mono * square, -mono]
        far = [turned(x) * wave for x in load] + [jnp.zeros((32, PAN), F32)]
        for at, side in enumerate((far, near)):
            rhs_ref[f, :, 2 * at * PAN : (2 * at + 1) * PAN] = jnp.concatenate(side, 0).astype(BF16)
            rhs_ref[f, :, (2 * at + 1) * PAN : (2 * at + 2) * PAN] = jnp.concatenate(
                [-turned(x) for x in side], 0
            ).astype(BF16)

    run(4, store_b, 0, 9, store_a, 0, 1, 2)
    run(2, store_a, 0, 13, store_b, 0, 9, 2)
    run(1, store_b, 0, 15, store_a, 0, 13, 2)
    run(1, mm_store=store_b, mm_slot=0, mm_block=15)
    run(1, mm_store=store_b, mm_slot=HELD // 2, mm_block=0)

    out_ref[...] = part_out[0].astype(F32)

    def finish(count, carry):
        step = NO - count
        place_copy(step).wait_send()
        part_copy(step).wait_send()
        part_copy(NO - step).wait_recv()
        out_ref[...] += part_in[step].astype(F32)
        return carry

    lax.fori_loop(1, NO, finish, 0)


def local(samples, panel_geom, panel_slot, observer_pos, observer_slot):
    vmem = pl.BlockSpec(memory_space=pltpu.VMEM)
    dma = pltpu.SemaphoreType.DMA
    out = pl.pallas_call(
        kernel,
        out_shape=jax.ShapeDtypeStruct((BINS * 2 * NF, OBS), F32),
        in_specs=[vmem] * 6,
        out_specs=vmem,
        scratch_shapes=[
            pltpu.VMEM((8, PAN), F32),
            pltpu.VMEM((8, PAN), F32),
            pltpu.VMEM((PAN, 128), BF16),
            pltpu.VMEM((NO, 8, OBS), F32),
            pltpu.VMEM((NO, 8, OBS), F32),
            pltpu.VMEM((NO, 64, OBS), BF16),
            pltpu.VMEM((256, OBS), F32),
            pltpu.VMEM((NF, 32, PAN), BF16),
            pltpu.VMEM((NF, 32, PAN), BF16),
            pltpu.VMEM((BINS, GROUPS, ROWS), BF16),
            pltpu.VMEM((HELD, BINS, ROWS, OBS), BF16),
            pltpu.VMEM((HELD // 2 + 1, BINS, ROWS, OBS), BF16),
            pltpu.VMEM((NO, 128, OBS), BF16),
            pltpu.VMEM((NO, 128, OBS), BF16),
            dma((NO,)),
            dma((NO,)),
            dma((NF,)),
            dma((NF,)),
            dma((NO,)),
            dma((NO,)),
        ],
        compiler_params=pltpu.CompilerParams(
            collective_id=0, has_side_effects=True, vmem_limit_bytes=63 * 2**20
        ),
    )(jnp.asarray(dft_table()), samples, panel_geom, panel_slot, observer_pos, observer_slot)
    return out.reshape(BINS, 2, NF, OBS).transpose(3, 0, 1, 2)


def solution(mesh):
    placed = (
        P(None, "freq", "obs"),
        P(None, "obs"),
        P("obs", None),
        P(None, "obs"),
        P("obs", None),
    )
    return jax.shard_map(
        local, mesh=mesh, in_specs=placed, out_specs=P("obs", "freq", None, None), check_vma=False
    )
```

```python
import functools
import math

import jax
import jax.numpy as jnp
import numpy as np
from jax import lax
from jax.experimental import pallas as pl
from jax.experimental.pallas import tpu as pltpu
from jax.sharding import PartitionSpec as P

WIN = 128
FREQS = 64
NF = 16
NO = 16
BINS = 4
PAN = 512
OBS = 256
CH = 4
HELD = 8
ROWS = 4 * PAN
GROUPS = 160
SUB = 16
F32 = jnp.float32
BF16 = jnp.bfloat16
MESH = pl.DeviceIdType.MESH

SIN_POLY = (4.4428797, -7.3078165, 3.5977743, -0.7911994)
COS_POLY = (1.414204, -6.9776373, 5.715188, -1.7282139)
STEP_POLY = (9.9999505e-01, -3.1246377e-02, 1.6224394e-04, -3.1450108e-07)


def dft_table():
    steps = np.arange(WIN, dtype=np.int32)
    bins = np.arange(1, FREQS + 1, dtype=np.int32)
    angles = np.float32(2.0 * math.pi / WIN) * (bins[:, None] * steps[None, :] % WIN).astype(np.float32)
    hann = np.float32(0.5) - np.float32(0.5) * np.cos(np.float32(2.0 * math.pi / WIN) * steps.astype(np.float32))
    weighted = hann[None, :] * (np.float32(1.0) / np.sqrt(np.sum(hann * hann)))
    parts = np.stack([np.cos(angles) * weighted, -np.sin(angles) * weighted], 1)
    return parts.reshape(2 * FREQS, WIN).astype(jnp.bfloat16)


def poly(coefs, x):
    total = coefs[-1] * x + coefs[-2]
    for coef in coefs[-3::-1]:
        total = total * x + coef
    return total


def pieces(x):
    first = x.astype(BF16).astype(F32)
    rest = x - first
    second = rest.astype(BF16).astype(F32)
    return first, second, (rest - second).astype(BF16).astype(F32)


def permuted(array, slot):
    n = array.shape[1]
    hot = (lax.broadcasted_iota(jnp.int32, (n, n), 0) == slot).astype(F32).astype(BF16)
    stacked = jnp.concatenate(pieces(array), 0).astype(BF16)
    picked = jnp.dot(stacked, hot, preferred_element_type=F32)
    return picked[0:8] + picked[8:16] + picked[16:24]


def norm(rows):
    return rows[0:1] * rows[0:1] + rows[1:2] * rows[1:2] + rows[2:3] * rows[2:3]


def tile_part(d2, step_poly):
    inverse = lax.rsqrt(d2)
    turns = d2 * inverse
    turns = turns - ((turns + 12582912.0) - 12582912.0)
    square = turns * turns
    sine = turns * poly(SIN_POLY, square)
    cosine = poly(COS_POLY, square)
    amp = inverse * inverse
    scaled = amp * sine
    c1 = amp - scaled * sine
    s1 = scaled * cosine
    step_cos = poly(step_poly, d2)
    rest = 1.0 - step_cos * step_cos
    step_sin = rest * lax.rsqrt(rest)
    cc, ss, sc, cs = c1 * step_cos, s1 * step_sin, s1 * step_cos, c1 * step_sin
    c0, c2 = cc + ss, cc - ss
    s0, s2 = sc - cs, sc + cs
    twice = step_cos + step_cos
    c3 = twice * c2 - c1
    s3 = twice * s2 - s1
    return ((c0, s0), (c1, s1), (c2, s2), (c3, s3)), inverse


def generate(store, k, quarter, d2_ref, step_poly):
    def one(sub, carry):
        base = pl.multiple_of(quarter * 128 + sub * SUB, SUB)
        d2 = d2_ref[pl.ds(pl.multiple_of(sub * SUB, SUB), SUB), :]
        factors, inverse = tile_part(d2, step_poly)
        for f in range(BINS):
            c, s = factors[f]
            for at, part in enumerate((c, s, c * inverse, s * inverse)):
                store[k, f, pl.ds(pl.multiple_of(base + at * PAN, SUB), SUB), :] = part.astype(BF16)
        return carry

    lax.fori_loop(0, 128 // SUB, one, 0, unroll=True)


def contract(store, k, f, rhs_ref, place_ref, block):
    out = jnp.dot(rhs_ref[f], store[k, f], preferred_element_type=F32)
    place = place_ref[block]
    return (
        out[0:32] * place[0:1]
        + out[32:64] * place[1:2]
        + out[64:96] * place[2:3]
        + out[96:128]
        + out[128:160] * place[3:4]
    )


def kernel(
    table_ref,
    samples_ref,
    geom_ref,
    slot_ref,
    pos_ref,
    pos_slot_ref,
    out_ref,
    eight,
    geometry,
    left,
    place_in,
    place,
    right,
    d2_ref,
    spec_out,
    spec_in,
    rhs_ref,
    store_a,
    store_b,
    part_out,
    part_in,
    place_send,
    place_recv,
    spec_send,
    spec_recv,
    part_send,
    part_recv,
):
    q = lax.axis_index("freq")
    me = lax.axis_index("obs")

    barrier = pltpu.get_barrier_semaphore()

    def greet(step, carry):
        pl.semaphore_signal(barrier, inc=1, device_id=(q, lax.rem(me + step, NO)), device_id_type=MESH)
        pl.semaphore_signal(barrier, inc=1, device_id=(lax.rem(q + step, NF), me), device_id_type=MESH)
        return carry

    lax.fori_loop(1, NO, greet, 0)

    eight[...] = jnp.zeros_like(eight)
    eight[0:3, 0:OBS] = pos_ref[...]
    seen = permuted(eight[:, 0:OBS], pos_slot_ref[...])
    place_in[0] = seen

    def place_copy(step):
        return pltpu.make_async_remote_copy(
            src_ref=place_in.at[0],
            dst_ref=place_in.at[NO - step],
            send_sem=place_send.at[step],
            recv_sem=place_recv.at[NO - step],
            device_id=(q, lax.rem(me + step, NO)),
            device_id_type=MESH,
        )

    def spec_copy(step):
        owner = lax.rem(q + step, NF)
        return pltpu.make_async_remote_copy(
            src_ref=spec_out.at[owner],
            dst_ref=spec_in.at[q],
            send_sem=spec_send.at[step],
            recv_sem=spec_recv.at[NF - step],
            device_id=(owner, me),
            device_id_type=MESH,
        )

    def part_copy(step):
        return pltpu.make_async_remote_copy(
            src_ref=part_out.at[step],
            dst_ref=part_in.at[NO - step],
            send_sem=part_send.at[step],
            recv_sem=part_recv.at[NO - step],
            device_id=(q, lax.rem(me + step, NO)),
            device_id_type=MESH,
        )

    def start_all(copy, first=1, last=NO):
        def one(step, carry):
            copy(NO - step).start()
            return carry

        lax.fori_loop(first, last, one, 0)

    for c in range(0, CH, 2):
        pair = [
            jnp.dot(table_ref[...], samples_ref[c + d], preferred_element_type=F32).reshape(NF, 2 * BINS, PAN)
            for d in range(2)
        ]
        spec_out[:, c * 8 : c * 8 + 16, :] = jnp.concatenate(pair, 1).astype(BF16)
    spec_in[q] = spec_out[q]

    eight[...] = jnp.zeros_like(eight)
    eight[0:4, :] = geom_ref[...]
    geometry[...] = permuted(eight[...], slot_ref[...])
    kappa = (q.astype(F32) + 0.5) * (0.5 / math.pi)
    scale = jnp.full((8, 1), kappa, F32)
    middle = jnp.sum(geometry[...], 1, keepdims=True) * (1.0 / PAN)
    geometry[0:3, :] = (geometry[0:3, :] - middle[0:3]) * scale[0:3]
    geo = geometry[...]
    eight[0:3, :] = -2.0 * geo[0:3]
    eight[3:4, :] = jnp.ones((1, PAN), F32)
    eight[4:5, :] = norm(geo)
    one, two, three = pieces(eight[...])
    side = jnp.concatenate([one, two, one, three, two, one, jnp.zeros((80, PAN), F32)], 0)
    left[...] = side.T.astype(BF16)

    def spread(block):
        seen = (place_in[block] - middle) * scale
        place[block] = seen
        place[block, 3:4, :] = norm(seen)
        place[block, 4:5, :] = jnp.ones((1, OBS), F32)
        one, two, three = pieces(place[block])
        right[block] = jnp.concatenate([one, one, two, one, two, three, jnp.zeros((16, OBS), F32)], 0).astype(BF16)

    def distances(turn):
        block, half = turn // 2, lax.rem(turn, 2)
        d2_ref[...] = jnp.dot(
            left[pl.ds(pl.multiple_of(half * 256, 256), 256), 0:64], right[block], preferred_element_type=F32
        )

    inverse_square = 1.0 / (kappa * kappa)
    step_poly = [jnp.float32(STEP_POLY[0])]
    power = jnp.float32(1.0)
    for coef in STEP_POLY[1:]:
        power = power * inverse_square
        step_poly.append(coef * power)

    def await_place(block):
        place_copy(NO - block).wait_recv()
        spread(block)

    def run(count, gen_store=None, gen_slot=0, gen_block=0, mm_store=None, mm_slot=0, mm_block=0, mm_count=1):
        def block_step(k, carry):
            def half_step(half, inner):
                if mm_store is None and gen_block > 0:
                    @pl.when(half == 1)
                    def _():
                        await_place(gen_block + k + 1)

                for h in range(2):
                    f = half * 2 + h
                    if mm_store is not None:
                        for m in range(mm_count):
                            at = k * mm_count + m
                            result = contract(mm_store, mm_slot + at, f, rhs_ref, place, mm_block + at)
                            part_out[mm_block + at, pl.ds(pl.multiple_of(f * 32, 32), 32), :] = result.astype(BF16)
                    if gen_store is not None:
                        generate(gen_store, gen_slot + k, f, d2_ref.at[h * 128:h * 128 + 128], step_poly)
                if gen_store is not None:
                    turn = (gen_block + k) * 2 + half
                    distances(jnp.minimum(turn + 1, 1 if gen_block == 0 else 2 * NO - 1))
                return inner

            lax.fori_loop(0, 2, half_step, 0)
            if mm_store is not None and mm_block > 0:
                for m in range(mm_count):
                    part_copy(mm_block + k * mm_count + m).start()
            return carry

        lax.fori_loop(0, count, block_step, 0)

    spread(0)

    row = lax.broadcasted_iota(jnp.int32, (PAN, PAN), 0)
    col = lax.broadcasted_iota(jnp.int32, (PAN, PAN), 1)
    source = (row & 15) * 32 + ((row >> 5) & 3) * 8 + (row >> 7) * 2 + ((row >> 4) & 1)
    perm = (source == col).astype(F32).astype(BF16)
    for side in range(2):
        store_b[0, side, 0:PAN, :] = perm[:, side * 256 : side * 256 + 256]

    distances(jnp.int32(0))
    run(1, store_b, HELD // 2)

    pl.semaphore_wait(barrier, NO - 1 + NF - 1)
    start_all(place_copy, 1, 4)
    start_all(spec_copy)
    start_all(place_copy, 4, NO)
    await_place(1)
    distances(jnp.int32(2))
    run(HELD, store_a, 0, 1)

    def await_rest(step, carry):
        await_place(step)
        return carry

    lax.fori_loop(HELD + 2, NO, await_rest, 0)

    def await_spec(step, carry):
        spec_copy(step).wait_send()
        spec_copy(NF - step).wait_recv()
        return carry

    lax.fori_loop(1, NF, await_spec, 0)

    def turned(x):
        return jnp.concatenate([-x[16:32], x[0:16]], 0)

    geo = geometry[...]
    weight = geo[3:4] * (0.25 / math.pi / math.sqrt(PAN * NO)) * (kappa * kappa)
    square = norm(geo)
    everything = spec_in[...].reshape(PAN, PAN)
    for f in range(BINS):
        wave = (q * BINS + (f + 1)).astype(F32) * 0.25 / kappa
        perm = jnp.concatenate([store_b[0, side, f * 128 : f * 128 + 128, :] for side in range(2)], 1)
        rows = jnp.dot(perm, everything, preferred_element_type=F32) * weight
        mono = turned(rows[0:32]) * wave
        load = [rows[32 * j + 32 : 32 * j + 64] for j in range(3)]
        load.append(-(load[0] * geo[0:1] + load[1] * geo[1:2] + load[2] * geo[2:3]))
        near = [load[j] + mono * (2.0 * geo[j : j + 1]) for j in range(3)] + [load[3] - mono * square, -mono]
        far = [turned(x) * wave for x in load] + [jnp.zeros((32, PAN), F32)]
        for at, side in enumerate((far, near)):
            rhs_ref[f, :, 2 * at * PAN : (2 * at + 1) * PAN] = jnp.concatenate(side, 0).astype(BF16)
            rhs_ref[f, :, (2 * at + 1) * PAN : (2 * at + 2) * PAN] = jnp.concatenate(
                [-turned(x) for x in side], 0
            ).astype(BF16)

    run(4, store_b, 0, 9, store_a, 0, 1, 2)
    run(2, store_a, 0, 13, store_b, 0, 9, 2)
    run(1, store_b, 0, 15, store_a, 0, 13, 2)
    run(1, mm_store=store_b, mm_slot=0, mm_block=15)
    run(1, mm_store=store_b, mm_slot=HELD // 2, mm_block=0)

    out_ref[...] = part_out[0].astype(F32)

    def finish(count, carry):
        step = NO - count
        place_copy(step).wait_send()
        part_copy(step).wait_send()
        part_copy(NO - step).wait_recv()
        out_ref[...] += part_in[step].astype(F32)
        return carry

    lax.fori_loop(1, NO, finish, 0)


def local(samples, panel_geom, panel_slot, observer_pos, observer_slot):
    vmem = pl.BlockSpec(memory_space=pltpu.VMEM)
    dma = pltpu.SemaphoreType.DMA
    out = pl.pallas_call(
        kernel,
        out_shape=jax.ShapeDtypeStruct((BINS * 2 * NF, OBS), F32),
        in_specs=[vmem] * 6,
        out_specs=vmem,
        scratch_shapes=[
            pltpu.VMEM((8, PAN), F32),
            pltpu.VMEM((8, PAN), F32),
            pltpu.VMEM((PAN, 128), BF16),
            pltpu.VMEM((NO, 8, OBS), F32),
            pltpu.VMEM((NO, 8, OBS), F32),
            pltpu.VMEM((NO, 64, OBS), BF16),
            pltpu.VMEM((256, OBS), F32),
            pltpu.VMEM((NF, 32, PAN), BF16),
            pltpu.VMEM((NF, 32, PAN), BF16),
            pltpu.VMEM((BINS, GROUPS, ROWS), BF16),
            pltpu.VMEM((HELD, BINS, ROWS, OBS), BF16),
            pltpu.VMEM((HELD // 2 + 1, BINS, ROWS, OBS), BF16),
            pltpu.VMEM((NO, 128, OBS), BF16),
            pltpu.VMEM((NO, 128, OBS), BF16),
            dma((NO,)),
            dma((NO,)),
            dma((NF,)),
            dma((NF,)),
            dma((NO,)),
            dma((NO,)),
        ],
        compiler_params=pltpu.CompilerParams(
            collective_id=0, has_side_effects=True, vmem_limit_bytes=63 * 2**20
        ),
    )(jnp.asarray(dft_table()), samples, panel_geom, panel_slot, observer_pos, observer_slot)
    return out.reshape(BINS, 2, NF, OBS).transpose(3, 0, 1, 2)


def solution(mesh):
    placed = (
        P(None, "freq", "obs"),
        P(None, "obs"),
        P("obs", None),
        P(None, "obs"),
        P("obs", None),
    )
    return jax.shard_map(
        local, mesh=mesh, in_specs=placed, out_specs=P("obs", "freq", None, None), check_vma=False
    )
```
